32 devices in a mesh: gx: 4 (over y, x), gy: 2 (over core), gz: 4 (over z).
Axes of the slice: x: 2, y: 2, z: 4, core: 2. Of those that a mesh axis runs over, the one named last changes fastest.
Arguments:
- earlier_edge_voltage: float32 [6, 32, 32, 1024], P(None, 'gx', 'gy', 'gz'), may hold values from -6 to 6
- coil_drive_current: float32 [6, 32, 32, 1024], P(None, 'gx', 'gy', 'gz'), may hold values from -18 to 18
- sigma_omega_cellwise: float32 [32, 32, 1024], P('gx', 'gy', 'gz'), may hold values from 0.2 to 3
- subdomain_inverse_full: bfloat16 [4, 2, 4, 16, 512, 512], P('gx', 'gy', 'gz'), may hold values from -0.25 to 0.25
- subdomain_inverse_main: float32 [4, 2, 4, 16, 512], P('gx', 'gy', 'gz'), may hold values from 0.25 to 1.75
- subdomain_layer_counts: int32 [4, 2, 4, 16], P('gx', 'gy', 'gz'), may hold values from 1 to 19, 256 in all within a row
- heat_layer_lookup: int32 [4, 8], P('gz'), may hold values from 1 to 96, 256 in all within a row
- warming_amount: float32 [4, 2, 4, 96, 32, 32], P('gx', 'gy', 'gz'), may hold values from 0 to 2
- heat_spreading_coef: float32 [4, 2, 4, 96, 32, 32], P('gx', 'gy', 'gz'), may hold values from 0.25 to 1
Outputs:
- field_new: float32 [6, 32, 32, 1024], P(None, 'gx', 'gy', 'gz')
- renewed_heat_rise: float32 [4, 2, 4, 96, 32, 32], P('gx', 'gy', 'gz')
- renewed_sigma_omega: float32 [32, 32, 1024], P('gx', 'gy', 'gz')
The draws below stay inside these ranges and needn't reach their ends.
Inputs may be any that keep to these rules, and one draw needn't show every extreme that they name: `subdomain_layer_counts`: each device's 16 segment lengths sum to 256, and every device has a segment of exactly 19 planes. `heat_layer_lookup`: each row sums to 256, and every row has a slab of exactly 96 planes.
All inputs are finite; a program needn't handle non-finite values.
Results may differ from the reference program's by a relative error of at most 0.013.
Values sent between devices are 32-bit elements; how exact they have to be, the bound alone decides.
A program may use at most 128 MiB of HBM per device.

```python
import math
import jax
import jax.numpy as jnp
import numpy as np
from jax import lax

CX = 8
CY = 16
CZ = 256
NSEG = 16
BLK = 512
SWEEPS = 2
SECTIONS = 4
MAXSEG = 19
NTH = 8
LAYER_CAP_HEAT = 96
VOXELS_ALONG_X = 32
VOXELS_ALONG_Y = 32
NZ = 1024
N_GX = 4
N_GY = 2
N_GZ = 4


def level_of(stream_key, extent, pieces, least, top_value):
    level, own = 1.0, jax.random.fold_in(stream_key, 6)
    for axis_at, blocks in pieces:
        heights = jnp.exp(jax.random.uniform(jax.random.fold_in(own, axis_at), (blocks,), jnp.float32, least / len(pieces), top_value / len(pieces)))
        level = level * jnp.repeat(heights, extent[axis_at] // blocks).reshape([-1 if axis == axis_at else 1 for axis in range(len(extent))])
    return level


def profile(number_of, total, limit, slope):
    loads = [(1 << 20) // math.isqrt(rank ** slope) + 1 for rank in range(2, number_of + 1)]
    spare, counts = total - limit - (number_of - 1), [1] * (number_of - 1)
    while spare > 0:
        movable = [i for i in range(number_of - 1) if counts[i] < limit]
        mass, left = sum([loads[i] for i in movable]), spare
        for i in movable:
            more = min(limit - counts[i], max(1, left * loads[i] // mass), spare)
            counts[i] = counts[i] + more
            spare = spare - more
    return np.array([limit] + counts)


def ragged(key, count, total, limit, lean):
    if count == 2:
        one = jax.random.randint(key, (), max(1, total - limit), min(limit, total - 1) + 1)
        return jnp.stack([one, total - one])
    lengths = jnp.asarray(profile(count, total, limit, lean), jnp.int32)
    couples = (count - 1) // 2
    giver, taker = lengths[1:1 + 2 * couples:2], lengths[2:2 + 2 * couples:2]
    slack = jnp.minimum(giver - 1, limit - taker)
    passed = jax.random.randint(jax.random.fold_in(key, 1), (couples,), 0, 1 << 20) % (slack + 1)
    lengths = lengths.at[1:1 + 2 * couples:2].set(giver - passed).at[2:2 + 2 * couples:2].set(taker + passed)
    return lengths[jax.random.permutation(jax.random.fold_in(key, 2), count)]


def normal_values(rng, dims, deviation, bound, shards=(), kind=jnp.bfloat16):
    loudness = level_of(rng, dims, shards, -0.22, 0.18) if shards else 1.0
    result = jax.random.normal(rng, dims, jnp.float32) * deviation * loudness
    return jnp.minimum(jnp.maximum(result, -bound), bound).astype(kind)


def setup_inputs(seed: int = 0) -> dict:
    key_list = jax.random.split(jax.random.key(seed), 10)
    earlier_edge_voltage = normal_values(key_list[0], (6, VOXELS_ALONG_X, VOXELS_ALONG_Y, NZ), 1.0, 6.0, ((1, 4), (2, 2), (3, 4)), jnp.float32)
    coil_drive_current = normal_values(key_list[1], (6, VOXELS_ALONG_X, VOXELS_ALONG_Y, NZ), 3.0, 18.0, ((1, 4), (2, 2), (3, 4)), jnp.float32)
    sigma_omega_cellwise = jnp.clip(jnp.exp(math.log(3.0) - 2.7080502 * jax.random.uniform(key_list[2], (VOXELS_ALONG_X, VOXELS_ALONG_Y, NZ), jnp.float32) ** level_of(key_list[2], (VOXELS_ALONG_X, VOXELS_ALONG_Y, NZ), ((0, 4), (1, 2), (2, 4)), -0.2, 0.2)), 0.2, 3.0)
    subdomain_inverse_full = normal_values(key_list[3], (N_GX, N_GY, N_GZ, NSEG, BLK, BLK), BLK ** -0.5, 0.25, ((0, 4), (1, 2), (2, 4)))
    subdomain_inverse_main = jnp.clip(1.0 + 0.15 * jax.random.normal(key_list[4], (N_GX, N_GY, N_GZ, NSEG, BLK), jnp.float32), 0.25, 1.75)
    subdomain_layer_counts = jax.vmap(lambda own: ragged(own, NSEG, CZ, MAXSEG, 1))(jax.random.split(key_list[5], N_GX * N_GY * N_GZ)).reshape((N_GX, N_GY, N_GZ, NSEG)).astype(jnp.int32)
    heat_layer_lookup = jax.vmap(lambda own: ragged(own, NTH, CZ, LAYER_CAP_HEAT, 2))(jax.random.split(key_list[6], N_GZ)).reshape((N_GZ, NTH)).astype(jnp.int32)
    warming_amount = jnp.clip(2.0 * jax.random.uniform(key_list[7], (N_GX, N_GY, N_GZ, LAYER_CAP_HEAT, VOXELS_ALONG_X, VOXELS_ALONG_Y), jnp.float32) ** level_of(key_list[7], (N_GX, N_GY, N_GZ, LAYER_CAP_HEAT, VOXELS_ALONG_X, VOXELS_ALONG_Y), ((0, 4), (1, 2), (2, 4)), -0.2, 0.2), 0.0, 2.0)
    heat_spreading_coef = jnp.clip(jnp.exp(math.log(1.0) - 1.3862944 * jax.random.uniform(key_list[8], (N_GX, N_GY, N_GZ, LAYER_CAP_HEAT, VOXELS_ALONG_X, VOXELS_ALONG_Y), jnp.float32) ** level_of(key_list[8], (N_GX, N_GY, N_GZ, LAYER_CAP_HEAT, VOXELS_ALONG_X, VOXELS_ALONG_Y), ((0, 4), (1, 2), (2, 4)), -0.2, 0.2)), 0.25, 1.0)
    return {"earlier_edge_voltage": earlier_edge_voltage, "coil_drive_current": coil_drive_current, "sigma_omega_cellwise": sigma_omega_cellwise, "subdomain_inverse_full": subdomain_inverse_full, "subdomain_inverse_main": subdomain_inverse_main, "subdomain_layer_counts": subdomain_layer_counts, "heat_layer_lookup": heat_layer_lookup, "warming_amount": warming_amount, "heat_spreading_coef": heat_spreading_coef}


mass_shift = 1.0
solver_scale = 0.2
coupling_scale = 0.05
time_step = 2.5
heat_drop = 0.15


def curl_curl(padded, conduct):
    size_x = padded.shape[1] - 2
    size_y = padded.shape[2] - 2
    size_z = padded.shape[3] - 2
    vector_parts_count = padded.reshape(2, 3, size_x + 2, size_y + 2, size_z + 2)
    field_x = vector_parts_count[:, 0]
    field_y = vector_parts_count[:, 1]
    field_z = vector_parts_count[:, 2]

    def wide_cut(array, shift_x, shift_y, shift_z):
        return array[:, shift_x:shift_x + size_x + 1, shift_y:shift_y + size_y + 1, shift_z:shift_z + size_z + 1]

    def core_cut(array, shift_x, shift_y, shift_z):
        return array[:, shift_x:shift_x + size_x, shift_y:shift_y + size_y, shift_z:shift_z + size_z]

    face_x = wide_cut(field_z, 0, 1, 0) - wide_cut(field_z, 0, 0, 0) - wide_cut(field_y, 0, 0, 1) + wide_cut(field_y, 0, 0, 0)
    face_y = wide_cut(field_x, 0, 0, 1) - wide_cut(field_x, 0, 0, 0) - wide_cut(field_z, 1, 0, 0) + wide_cut(field_z, 0, 0, 0)
    face_z = wide_cut(field_y, 1, 0, 0) - wide_cut(field_y, 0, 0, 0) - wide_cut(field_x, 0, 1, 0) + wide_cut(field_x, 0, 0, 0)
    curl_x = core_cut(face_z, 1, 1, 1) - core_cut(face_z, 1, 0, 1) - core_cut(face_y, 1, 1, 1) + core_cut(face_y, 1, 1, 0)
    curl_y = core_cut(face_x, 1, 1, 1) - core_cut(face_x, 1, 1, 0) - core_cut(face_z, 1, 1, 1) + core_cut(face_z, 0, 1, 1)
    curl_z = core_cut(face_y, 1, 1, 1) - core_cut(face_y, 0, 1, 1) - core_cut(face_x, 1, 1, 1) + core_cut(face_x, 1, 0, 1)
    curl_all = jnp.stack([curl_x, curl_y, curl_z], axis=1)
    center = vector_parts_count[:, :, 1:-1, 1:-1, 1:-1]
    real_part = curl_all[0] + mass_shift * center[0] - conduct * center[1]
    imag_part = curl_all[1] + mass_shift * center[1] + conduct * center[0]
    return jnp.concatenate([real_part, imag_part], axis=0)


def block_correction(residual, solvers, diagonal, seg_len):
    seg_count = diagonal.shape[0]
    block_width = diagonal.shape[1]
    extent_x = residual.shape[1]
    extent_y = residual.shape[2]
    extent_z = residual.shape[3]
    window_planes = block_width // 24
    used_width = window_planes * 24
    column_x = extent_x // 2
    column_y = extent_y // 2
    starts = (jnp.cumsum(seg_len) - seg_len).astype(jnp.int32)
    offsets = jnp.arange(window_planes, dtype=jnp.int32)
    planes = (starts[:, None] - 1 + offsets[None, :]).astype(jnp.int32)
    inside = (offsets[None, :] <= seg_len[:, None] + 1) & (planes >= 0) & (planes < extent_z)
    plane_rows = jnp.transpose(residual, (3, 0, 1, 2)).reshape(extent_z, 6 * extent_x * extent_y)
    picked = plane_rows[jnp.clip(planes, 0, extent_z - 1)] * inside[:, :, None].astype(jnp.float32)
    picked = picked.reshape(seg_count, window_planes, 6, column_x, 2, column_y, 2)
    picked = jnp.transpose(picked, (0, 3, 5, 1, 2, 4, 6)).reshape(seg_count, column_x * column_y, used_width)
    vectors = jnp.pad(picked, ((0, 0), (0, 0), (0, block_width - used_width))).astype(jnp.bfloat16)
    product = jnp.einsum("sij,scj->sci", solvers.astype(jnp.float32), vectors.astype(jnp.float32))
    solved = coupling_scale * product + solver_scale * diagonal[:, None, :] * vectors.astype(jnp.float32)
    restored = solved[:, :, :used_width].reshape(seg_count, column_x, column_y, window_planes, 6, 2, 2)
    restored = jnp.transpose(restored, (0, 3, 4, 1, 5, 2, 6)).reshape(seg_count * window_planes, 6 * extent_x * extent_y)
    plane_ids = jnp.arange(extent_z, dtype=jnp.int32)
    owner_seg = jnp.sum((starts[None, :] <= plane_ids[:, None]).astype(jnp.int32), axis=1) - 1
    seg_ids = jnp.arange(seg_count, dtype=jnp.int32)
    own_start = jnp.sum(jnp.where(owner_seg[:, None] == seg_ids[None, :], starts[None, :], 0), axis=1)
    slots = (owner_seg * window_planes + plane_ids - own_start + 1).astype(jnp.int32)
    gathered = restored[slots]
    return jnp.transpose(gathered.reshape(extent_z, 6, extent_x, extent_y), (1, 2, 3, 0))


def to_devices(whole):
    shaped = whole.reshape(6, N_GX, CX, N_GY, CY, N_GZ, CZ)
    return jnp.transpose(shaped, (1, 3, 5, 0, 2, 4, 6)).reshape(N_GX * N_GY * N_GZ, 6, CX, CY, CZ)


def from_devices(device_parts):
    shaped = device_parts.reshape(N_GX, N_GY, N_GZ, 6, CX, CY, CZ)
    return jnp.transpose(shaped, (3, 0, 4, 1, 5, 2, 6)).reshape(6, VOXELS_ALONG_X, VOXELS_ALONG_Y, NZ)


def heat_rate(values, rates, joule_z):
    padded = jnp.pad(values, 1)
    beside_all = padded[2:, 1:-1, 1:-1] + padded[:-2, 1:-1, 1:-1]
    beside_all = beside_all + padded[1:-1, 2:, 1:-1] + padded[1:-1, :-2, 1:-1]
    beside_all = beside_all + padded[1:-1, 1:-1, 2:] + padded[1:-1, 1:-1, :-2]
    return rates * (beside_all - 6.0 * values) + joule_z


def reference(earlier_edge_voltage, coil_drive_current, sigma_omega_cellwise, subdomain_inverse_full, subdomain_inverse_main, subdomain_layer_counts, heat_layer_lookup, warming_amount, heat_spreading_coef):
    device_count = N_GX * N_GY * N_GZ
    solver_parts = subdomain_inverse_full.reshape(device_count, NSEG, BLK, BLK)
    diagonal_parts = subdomain_inverse_main.reshape(device_count, NSEG, BLK)
    length_parts = subdomain_layer_counts.reshape(device_count, NSEG)

    def one_device(device_items):
        return block_correction(device_items[0], device_items[1], device_items[2], device_items[3])

    vector_parts_count = earlier_edge_voltage
    for sweep_index in range(SWEEPS):
        padded = jnp.pad(vector_parts_count, ((0, 0), (1, 1), (1, 1), (1, 1)))
        residual = coil_drive_current - curl_curl(padded, sigma_omega_cellwise)
        corrections = lax.map(one_device, (to_devices(residual), solver_parts, diagonal_parts, length_parts))
        vector_parts_count = vector_parts_count + from_devices(corrections)
    joule_heat = 0.5 * sigma_omega_cellwise * jnp.sum(vector_parts_count * vector_parts_count, axis=0)

    slab_lengths = heat_layer_lookup
    slab_starts = (jnp.cumsum(slab_lengths, axis=1) - slab_lengths).astype(jnp.int32)
    offsets = jnp.arange(LAYER_CAP_HEAT, dtype=jnp.int32)
    range_ids = jnp.arange(N_GZ, dtype=jnp.int32)
    plane_index = (range_ids[:, None, None] * CZ + slab_starts[:, :, None] + offsets[None, None, :]).astype(jnp.int32)
    inside = offsets[None, None, :] < slab_lengths[:, :, None]
    local_planes = jnp.arange(CZ, dtype=jnp.int32)
    owner_slab = (jnp.sum((slab_starts[:, None, :] <= local_planes[None, :, None]).astype(jnp.int32), axis=2) - 1).astype(jnp.int32)
    owner_start = jnp.take_along_axis(slab_starts, owner_slab, axis=1)
    flat_index = ((range_ids[:, None] * NTH + owner_slab) * LAYER_CAP_HEAT + local_planes[None, :] - owner_start).reshape(NZ).astype(jnp.int32)

    def collect_onto_mesh(slabs):
        stacked = jnp.transpose(slabs, (2, 0, 1, 3, 4, 5)).reshape(N_GZ * NTH * LAYER_CAP_HEAT, VOXELS_ALONG_X, VOXELS_ALONG_Y)
        return stacked[flat_index]

    def distribute_onto_layers(whole):
        picked = whole[jnp.clip(plane_index, 0, NZ - 1)] * inside[:, :, :, None, None].astype(jnp.float32)
        return jnp.transpose(picked.reshape(N_GZ, N_GX, N_GY, LAYER_CAP_HEAT, VOXELS_ALONG_X, VOXELS_ALONG_Y), (1, 2, 0, 3, 4, 5))

    joule_z = jnp.transpose(joule_heat, (2, 0, 1))
    rates = collect_onto_mesh(heat_spreading_coef)
    section_coef = time_step / (SECTIONS * SECTIONS)
    earlier_estimate = collect_onto_mesh(warming_amount)
    current_estimate = earlier_estimate + section_coef * heat_rate(earlier_estimate, rates, joule_z)
    for section_index in range(2, SECTIONS + 1):
        following = 2.0 * current_estimate - earlier_estimate + 2.0 * section_coef * heat_rate(current_estimate, rates, joule_z)
        earlier_estimate = current_estimate
        current_estimate = following
    renewed_heat_rise = distribute_onto_layers(current_estimate)
    renewed_sigma_omega = sigma_omega_cellwise * jnp.exp(-heat_drop * jnp.transpose(current_estimate, (1, 2, 0)))
    return (vector_parts_count, renewed_heat_rise, renewed_sigma_omega)
```

```python
import functools

import jax
import jax.numpy as jnp
from jax import lax
from jax.experimental import pallas as pl
from jax.experimental.pallas import tpu as pltpu
from jax.sharding import PartitionSpec as P

SWEEPS = 2
SECTIONS = 4
MESH = pl.DeviceIdType.MESH

mass_shift = 1.0
solver_scale = 0.2
coupling_scale = 0.05
time_step = 2.5
heat_drop = 0.15

CHUNK = 64
PAD = 8


def roll(value, shift, axis):
    size = value.shape[axis]
    shift = shift % size
    return value if shift == 0 else pltpu.roll(value, shift, axis)


def remote(src, dst, ssem, rsem, device):
    return pltpu.make_async_remote_copy(
        src_ref=src,
        dst_ref=dst,
        send_sem=ssem,
        recv_sem=rsem,
        device_id=device,
        device_id_type=MESH,
    )


def when_all(entries, act):
    for there, item in entries:

        @pl.when(there)
        def _():
            act(item)


def start_all(entries):
    when_all(entries, lambda copy: copy.start())


def wait_sent(entries):
    when_all(entries, lambda copy: copy.wait_send())


def wait_got(entries):
    when_all(entries, lambda copy: copy.wait_recv())


def greet(entries, others=()):
    barrier = pltpu.get_barrier_semaphore()

    def signal(device):
        pl.semaphore_signal(barrier, inc=1, device_id=device, device_id_type=MESH)

    for device in others:
        signal(device)
    when_all(entries, signal)
    peers = sum([there.astype(jnp.int32) for there, _ in entries], jnp.int32(len(others)))
    pl.semaphore_wait(barrier, peers)


def residual_kernel(
    dims,
    e_ref,
    cur_ref,
    sig_ref,
    res_out,
    field,
    div,
    send_x,
    send_y,
    send_z,
    recv_x,
    recv_y,
    recv_z,
    dsend_x,
    dsend_y,
    dsend_z,
    drecv_x,
    drecv_y,
    drecv_z,
    face_send_sem,
    face_recv_sem,
    div_send_sem,
    div_recv_sem,
):
    gxc, gyc, gzc, cx, cy, cz, nseg, blk, cap = dims
    lanes = cx * cy
    chunks = cz // CHUNK
    gx, gy, gz = lax.axis_index("gx"), lax.axis_index("gy"), lax.axis_index("gz")
    f32 = jnp.float32

    sides = {
        "x+": (gx < gxc - 1, (gx + 1, gy, gz)),
        "x-": (gx > 0, (gx - 1, gy, gz)),
        "y+": (gy < gyc - 1, (gx, gy + 1, gz)),
        "y-": (gy > 0, (gx, gy - 1, gz)),
        "z+": (gz < gzc - 1, (gx, gy, gz + 1)),
        "z-": (gz > 0, (gx, gy, gz - 1)),
    }

    for ref in (recv_x, recv_y, recv_z, drecv_x, drecv_y, drecv_z, send_z, dsend_z):
        ref[...] = jnp.zeros_like(ref)

    for c in range(6):
        field[c, pl.ds(PAD, cz)] = e_ref[c]

    lane = lax.broadcasted_iota(jnp.int32, (CHUNK, lanes), 1)
    lane_x = lane // cy
    lane_y = lane % cy

    def face_copies():
        names = ["x+", "x-", "y+", "y-", "z+", "z-"]
        pairs = [
            (send_x.at[0], recv_x.at[0]),
            (send_x.at[1], recv_x.at[1]),
            (send_y.at[0], recv_y.at[0]),
            (send_y.at[1], recv_y.at[1]),
            (send_z.at[0], recv_z.at[0]),
            (send_z.at[1], recv_z.at[1]),
        ]
        copies = [
            remote(src, dst, face_send_sem.at[i], face_recv_sem.at[i], sides[n][1])
            for i, (n, (src, dst)) in enumerate(zip(names, pairs))
        ]
        sends = [(sides[n][0], copy) for n, copy in zip(names, copies)]
        back = ["x-", "x+", "y-", "y+", "z-", "z+"]
        gets = [(sides[n][0], copy) for n, copy in zip(back, copies)]
        return sends, gets

    def div_copies():
        names = ["x-", "y-", "z-"]
        pairs = [
            (dsend_x, drecv_x),
            (dsend_y, drecv_y),
            (dsend_z, drecv_z),
        ]
        copies = [
            remote(src, dst, div_send_sem.at[i], div_recv_sem.at[i], sides[n][1])
            for i, (n, (src, dst)) in enumerate(zip(names, pairs))
        ]
        sends = [(sides[n][0], copy) for n, copy in zip(names, copies)]
        gets = [(sides[n][0], copy) for n, copy in zip(["x+", "y+", "z+"], copies)]
        return sends, gets

    def pack_faces():
        @pl.loop(0, chunks)
        def _(i):
            rows = pl.ds(pl.multiple_of(i * CHUNK, CHUNK), CHUNK)
            inner = pl.ds(pl.multiple_of(i * CHUNK + PAD, 8), CHUNK)
            x_hi = jnp.zeros((CHUNK, lanes), f32)
            x_lo, y_hi, y_lo = x_hi, x_hi, x_hi
            for c in range(6):
                v = field[c, inner]
                here = lane_x == c
                x_hi = jnp.where(here, roll(v, cy * (c - cx + 1), 1), x_hi)
                x_lo = jnp.where(here, roll(v, cy * c, 1), x_lo)
                here = lane_y == c
                y_hi = jnp.where(here, roll(v, c - cy + 1, 1), y_hi)
                y_lo = jnp.where(here, roll(v, c, 1), y_lo)
            send_x[0, rows] = x_hi
            send_x[1, rows] = x_lo
            send_y[0, rows] = y_hi
            send_y[1, rows] = y_lo

        for c in range(6):
            send_z[0, pl.ds(c, 1)] = field[c, pl.ds(PAD + cz - 1, 1)]
            send_z[1, pl.ds(c, 1)] = field[c, pl.ds(PAD, 1)]

    pack_faces()
    greet(list(sides.values()))
    sends, gets = face_copies()
    start_all(sends)
    wait_got(gets)
    for c in range(6):
        field[c, pl.ds(PAD - 1, 1)] = recv_z[0, pl.ds(c, 1)]
        field[c, pl.ds(PAD + cz, 1)] = recv_z[1, pl.ds(c, 1)]

    def x_low(v, got, c):
        return jnp.where(lane_x == 0, roll(got, -cy * c, 1), roll(v, cy, 1))

    def x_high(v, got, c):
        return jnp.where(lane_x == cx - 1, roll(got, cy * (cx - 1 - c), 1), roll(v, -cy, 1))

    def y_low(v, got, c):
        return jnp.where(lane_y == 0, roll(got, -c, 1), roll(v, 1, 1))

    def y_high(v, got, c):
        return jnp.where(lane_y == cy - 1, roll(got, cy - 1 - c, 1), roll(v, -1, 1))

    for i in range(chunks):
        z0 = i * CHUNK
        rows = pl.ds(z0, CHUNK)
        for part in range(2):
            cs = [3 * part + k for k in range(3)]
            ex, ey, ez = [field[c, pl.ds(PAD + z0, CHUNK)] for c in cs]
            d = (
                ex
                - x_low(ex, recv_x[0, rows], cs[0])
                + ey
                - y_low(ey, recv_y[0, rows], cs[1])
                + ez
                - field[cs[2], pl.ds(PAD + z0 - 1, CHUNK)]
            )
            div[part, pl.ds(PAD + z0, CHUNK)] = d
            place = 2 * i + part
            dx = roll(d, cy * place, 1)
            dy = roll(d, place, 1)
            if place == 0:
                dsend_x[...] = dx
                dsend_y[...] = dy
            else:
                dsend_x[...] = jnp.where(lane_x == place, dx, dsend_x[...])
                dsend_y[...] = jnp.where(lane_y == place, dy, dsend_y[...])
    for part in range(2):
        dsend_z[pl.ds(part, 1)] = div[part, pl.ds(PAD, 1)]
    dsends, dgets = div_copies()
    start_all(dsends)
    wait_got(dgets)
    rim_z = jnp.where(gz == gzc - 1, 1.0, 0.0)
    for part in range(2):
        top = field[3 * part + 2, pl.ds(PAD + cz - 1, 1)]
        div[part, pl.ds(PAD + cz, 1)] = drecv_z[pl.ds(part, 1)] - rim_z * top

    rim = [
        jnp.where((lane_x == cx - 1) & (gx == gxc - 1), 1.0, 0.0),
        jnp.where((lane_y == cy - 1) & (gy == gyc - 1), 1.0, 0.0),
    ]

    for i in range(chunks):
        z0 = i * CHUNK
        rows = pl.ds(z0, CHUNK)
        sig = sig_ref[rows]
        for part in range(2):
            d = div[part, pl.ds(PAD + z0, CHUNK)]
            place = 2 * i + part
            ahead = [
                x_high(d, drecv_x[...], place),
                y_high(d, drecv_y[...], place),
                div[part, pl.ds(PAD + z0 + 1, CHUNK)],
            ]
            for k in range(3):
                c = 3 * part + k
                e = field[c, pl.ds(PAD + z0, CHUNK)]
                step = ahead[k] - d
                if k < 2:
                    step = step - rim[k] * e
                other = field[(c + 3) % 6, pl.ds(PAD + z0, CHUNK)]
                lap = (
                    x_low(e, recv_x[0, rows], c)
                    + x_high(e, recv_x[1, rows], c)
                    + y_low(e, recv_y[0, rows], c)
                    + y_high(e, recv_y[1, rows], c)
                    + field[c, pl.ds(PAD + z0 - 1, CHUNK)]
                    + field[c, pl.ds(PAD + z0 + 1, CHUNK)]
                    - 6.0 * e
                )
                turn = sig * other
                applied = step - lap + mass_shift * e
                applied = applied - turn if part == 0 else applied + turn
                res_out[c, rows] = cur_ref[c, rows] - applied
    wait_sent(sends)
    wait_sent(dsends)


def solve_kernel(
    dims,
    last,
    ints,
    e_ref,
    res_ref,
    mat_hbm,
    diag_ref,
    group_ref,
    *refs,
):
    gxc, gyc, gzc, cx, cy, cz, nseg, blk, cap = dims
    if last:
        sig_ref, field_out, heat_send, mats, wide, solved, planes, joule, mat_sem = refs
    else:
        field_out, mats, wide, solved, planes, mat_sem = refs
    owners = gxc * gyc
    lanes = cx * cy
    chunks = cz // CHUNK
    at_slot = 2 * nseg
    at_start = at_slot + cz
    f32 = jnp.float32

    copies = [
        pltpu.make_async_copy(mat_hbm.at[s], mats.at[s], mat_sem.at[s]) for s in range(nseg)
    ]
    for copy in copies:
        copy.start()

    lane = lax.broadcasted_iota(jnp.int32, (CHUNK, lanes), 1)
    pick_lane = (lane // cy % 2) * 2 + lane % cy % 2
    block_row = lax.broadcasted_iota(jnp.int32, (blk, lanes), 0)

    wide[pl.ds(0, 24)] = jnp.zeros((24, lanes), f32)
    tail = wide.shape[0] - (cz + 1) * 24
    wide[pl.ds((cz + 1) * 24, tail)] = jnp.zeros((tail, lanes), f32)
    for i in range(chunks):
        z0 = i * CHUNK
        for c in range(6):
            r = res_ref[c, pl.ds(z0, CHUNK)].astype(jnp.bfloat16)
            spread = jnp.dot(r, group_ref[...], preferred_element_type=f32)
            for pq in range(4):
                wide[pl.ds((z0 + 1) * 24 + c * 4 + pq, CHUNK, stride=24), :] = spread[
                    :, pq * lanes : (pq + 1) * lanes
                ]

    for s in range(nseg):
        base = pl.multiple_of(ints[s], 8)
        v = wide[pl.ds(base, blk), :]
        v = jnp.where(block_row < ints[nseg + s], v, 0.0)
        copies[s].wait()
        product = jnp.dot(mats[s], v.astype(jnp.bfloat16), preferred_element_type=f32)
        diag = solver_scale * diag_ref[:, s : s + 1]
        solved[pl.ds(s * blk, blk)] = coupling_scale * product + diag * v

    @pl.loop(0, cz // 8)
    def _(i):
        for j in range(8):
            z = i * 8 + j
            base = pl.multiple_of(ints[at_slot + z], 8)
            planes[pl.ds(pl.multiple_of(z * 24, 8), 24)] = solved[pl.ds(base, 24), :]

    for i in range(chunks):
        z0 = i * CHUNK
        rows = pl.ds(z0, CHUNK)
        total = jnp.zeros((CHUNK, lanes), f32)
        for c in range(6):
            first = z0 * 24 + c * 4
            v = planes[pl.ds(first, CHUNK, stride=24), :]
            for pq in range(1, 4):
                v = jnp.where(pick_lane == pq, planes[pl.ds(first + pq, CHUNK, stride=24), :], v)
            v = e_ref[c, rows] + v
            field_out[c, rows] = v
            total = total + v * v
        if last:
            joule[rows] = 0.5 * sig_ref[rows] * total

    if last:
        joule[pl.ds(cz, cap)] = jnp.zeros((cap, lanes), f32)
        for p in range(owners):
            heat_send[pl.ds(p * cap, cap)] = joule[pl.ds(ints[at_start + p], cap), :]


def heat_kernel(
    dims,
    heat_send,
    temp_ref,
    rate_ref,
    end_ref,
    heat_out,
    back_out,
    heat_recv,
    heat_src,
    state_a,
    state_b,
    end_send,
    end_recv,
    factors,
    back_send,
    back_recv,
    a2a_send_sem,
    a2a_recv_sem,
    end_send_sem,
    end_recv_sem,
):
    gxc, gyc, gzc, cx, cy, cz, nseg, blk, cap = dims
    owners = gxc * gyc
    lanes = cx * cy
    gx, gy, gz = lax.axis_index("gx"), lax.axis_index("gy"), lax.axis_index("gz")
    me = gx * gyc + gy
    f32 = jnp.float32

    last = owners - 1
    up_owner = jnp.where(me == last, 0, me + 1)
    up_gz = jnp.where(me == last, gz + 1, gz)
    down_owner = jnp.where(me == 0, last, me - 1)
    down_gz = jnp.where(me == 0, gz - 1, gz)
    chain = {
        "up": ((me < last) | (gz < gzc - 1), (up_owner // gyc, up_owner % gyc, up_gz)),
        "down": ((me > 0) | (gz > 0), (down_owner // gyc, down_owner % gyc, down_gz)),
    }
    end_recv[...] = jnp.zeros_like(end_recv)

    others = [lax.rem(me + step, owners) for step in range(1, owners)]
    cross_up = (me == last) & (gz < gzc - 1)
    cross_down = (me == 0) & (gz > 0)
    greet(
        [(cross_up, chain["up"][1]), (cross_down, chain["down"][1])],
        [(other // gyc, other % gyc, gz) for other in others],
    )

    def exchange(which, src, dst):
        copies = []
        for step in range(1, owners):
            other = lax.rem(me + step, owners)
            copies.append(
                remote(
                    src.at[pl.ds(pl.multiple_of(other * cap, 8), cap)],
                    dst.at[pl.ds(pl.multiple_of(me * cap, 8), cap)],
                    a2a_send_sem.at[which, step - 1],
                    a2a_recv_sem.at[which, step - 1],
                    (other // gyc, other % gyc, gz),
                )
            )
        for copy in copies:
            copy.start()
        return copies

    def ends(step):
        up = remote(
            end_send.at[step, 0],
            end_recv.at[step, 0],
            end_send_sem.at[step, 0],
            end_recv_sem.at[step, 0],
            chain["up"][1],
        )
        down = remote(
            end_send.at[step, 1],
            end_recv.at[step, 1],
            end_send_sem.at[step, 1],
            end_recv_sem.at[step, 1],
            chain["down"][1],
        )
        sends = [(chain["up"][0], up), (chain["down"][0], down)]
        gets = [(chain["down"][0], up), (chain["up"][0], down)]
        return sends, gets

    def send_ends(step, state):
        total = jnp.zeros((owners, lanes), f32)
        for o in range(0, cap, 8):
            total = total + jnp.sum(end_ref[pl.ds(o, 8)] * state[pl.ds(o + 1, 8)], axis=0)
        end_send[step, 0] = total
        end_send[step, 1] = state[1]
        sends, _ = ends(step)
        start_all(sends)

    mine = pl.ds(pl.multiple_of(me * cap, 8), cap)
    copies = exchange(0, heat_send, heat_recv)

    state_a[pl.ds(1, cap)] = temp_ref[...]
    for state in (state_a, state_b):
        state[0] = jnp.zeros((owners, lanes), f32)
        state[cap + 1] = jnp.zeros((owners, lanes), f32)
    send_ends(0, state_a)

    heat_recv[mine] = heat_send[mine]
    for copy in copies:
        copy.wait()
    for p in range(owners):
        heat_src[pl.ds(p, cap, stride=owners), :] = heat_recv[pl.ds(p * cap, cap)]

    group = 8
    shape = (group, owners, lanes)
    own = lax.broadcasted_iota(jnp.int32, shape, 1)
    at = lax.broadcasted_iota(jnp.int32, shape, 2)
    at_x, at_y = at // cy, at % cy
    own_y = own % gyc

    def beside(v):
        t = roll(v, cy, 2)
        u = jnp.where(own >= gyc, roll(t, gyc, 1), 0.0)
        total = jnp.where(at_x == 0, u, t)
        t = roll(v, -cy, 2)
        u = jnp.where(own < owners - gyc, roll(t, -gyc, 1), 0.0)
        total = total + jnp.where(at_x == cx - 1, u, t)
        u = jnp.where(own_y > 0, roll(roll(v, 1 - cy, 2), 1, 1), 0.0)
        total = total + jnp.where(at_y == 0, u, roll(v, 1, 2))
        u = jnp.where(own_y < gyc - 1, roll(roll(v, cy - 1, 2), -1, 1), 0.0)
        return total + jnp.where(at_y == cy - 1, u, roll(v, -1, 2))

    coef = time_step / (SECTIONS * SECTIONS)
    states = [state_a, state_b]
    for step in range(SECTIONS):
        now, to = states[step % 2], states[1 - step % 2]
        if step > 0:
            send_ends(step, now)
        sends, gets = ends(step)
        wait_got(gets)
        now[0] = end_recv[step, 0]

        @pl.loop(0, cap // group)
        def _(i):
            t0 = i * group
            v = now[pl.ds(t0 + 1, group)]
            above = jnp.broadcast_to(end_recv[step, 1][None], shape)
            end = end_ref[pl.ds(t0, group)]
            up = end * above + (1.0 - end) * now[pl.ds(t0 + 2, group)]
            rates = rate_ref[pl.ds(t0, group)]
            rows = pl.ds(pl.multiple_of(t0 * owners, 8), group * owners)
            heat = heat_src[rows].reshape(shape)
            rate = rates * (beside(v) + now[pl.ds(t0, group)] + up - 6.0 * v) + heat
            if step == 0:
                following = v + coef * rate
            else:
                following = 2.0 * v - to[pl.ds(t0 + 1, group)] + 2.0 * coef * rate
            to[pl.ds(t0 + 1, group)] = following
            if step == SECTIONS - 1:
                heat_out[pl.ds(t0, group)] = following
                factors[rows] = jnp.exp(-heat_drop * following).reshape(group * owners, lanes)

        wait_sent(sends)

    for p in range(owners):
        back_send[pl.ds(p * cap, cap)] = factors[pl.ds(p, cap, stride=owners), :]
    back_recv[mine] = back_send[mine]
    for copy in exchange(1, back_send, back_recv):
        copy.wait()
    back_out[...] = back_recv[...]


def body(
    mesh_shape,
    earlier_edge_voltage,
    coil_drive_current,
    sigma_omega_cellwise,
    subdomain_inverse_full,
    subdomain_inverse_main,
    subdomain_layer_counts,
    heat_layer_lookup,
    warming_amount,
    heat_spreading_coef,
):
    gxc, gyc, gzc = mesh_shape
    owners = gxc * gyc
    cx, cy, cz = sigma_omega_cellwise.shape
    lanes = cx * cy
    nseg, blk = subdomain_inverse_main.shape[3:]
    cap = warming_amount.shape[3]
    f32 = jnp.float32

    seg_len = subdomain_layer_counts[0, 0, 0]
    starts = jnp.cumsum(seg_len) - seg_len
    plane_ids = jnp.arange(cz, dtype=jnp.int32)
    owner_seg = jnp.sum((starts[None, :] <= plane_ids[:, None]).astype(jnp.int32), axis=1) - 1
    own_start = jnp.sum(
        jnp.where(owner_seg[:, None] == jnp.arange(nseg)[None, :], starts[None, :], 0), axis=1
    )
    slots = owner_seg * blk + (plane_ids - own_start + 1) * 24
    slab_len = heat_layer_lookup[0]
    slab_starts = jnp.cumsum(slab_len) - slab_len
    owner_slab = jnp.sum((slab_starts[None, :] <= plane_ids[:, None]).astype(jnp.int32), axis=1) - 1
    slab_start = jnp.sum(
        jnp.where(owner_slab[:, None] == jnp.arange(owners)[None, :], slab_starts[None, :], 0),
        axis=1,
    )
    back = owner_slab * cap + plane_ids - slab_start
    me = lax.axis_index("gx") * gyc + lax.axis_index("gy")
    my_len = jnp.sum(jnp.where(jnp.arange(owners) == me, slab_len, 0))
    ints = jnp.concatenate(
        [starts * 24, (seg_len + 2) * 24, slots, slab_starts]
    ).astype(jnp.int32)

    def planes_first(a):
        return jnp.swapaxes(a.reshape(-1, lanes, cz), 1, 2)

    def onto_tiles(a):
        a = a[0, 0, 0].reshape(cap, gxc, cx, gyc, cy)
        return jnp.transpose(a, (0, 1, 3, 2, 4)).reshape(cap, owners, lanes)

    diag = jnp.pad(subdomain_inverse_main[0, 0, 0].T, ((0, 0), (0, lanes - nseg)))
    source = jnp.arange(lanes)[:, None]
    target = jnp.arange(4 * lanes)[None, :]
    pq, to = target // lanes, target % lanes
    same = ((source // cy // 2) == (to // cy // 2)) & ((source % cy // 2) == (to % cy // 2))
    part = (source // cy % 2) * 2 + source % cy % 2
    group = (same & (part == pq)).astype(jnp.bfloat16)

    vmem = pl.BlockSpec(memory_space=pltpu.VMEM)
    smem = pl.BlockSpec(memory_space=pltpu.SMEM)
    hbm = pl.BlockSpec(memory_space=pl.ANY)
    dims = (gxc, gyc, gzc, cx, cy, cz, nseg, blk, cap)
    whole = jax.ShapeDtypeStruct((6, cz, lanes), f32)
    slabs = jax.ShapeDtypeStruct((owners * cap, lanes), f32)
    dma = pltpu.SemaphoreType.DMA

    def residual(field, sweep):
        return pl.pallas_call(
            functools.partial(residual_kernel, dims),
            out_shape=whole,
            in_specs=[vmem] * 3,
            out_specs=vmem,
            scratch_shapes=[
                pltpu.VMEM((6, cz + 2 * PAD, lanes), f32),
                pltpu.VMEM((2, cz + 2 * PAD, lanes), f32),
                pltpu.VMEM((2, cz, lanes), f32),
                pltpu.VMEM((2, cz, lanes), f32),
                pltpu.VMEM((2, 8, lanes), f32),
                pltpu.VMEM((2, cz, lanes), f32),
                pltpu.VMEM((2, cz, lanes), f32),
                pltpu.VMEM((2, 8, lanes), f32),
                pltpu.VMEM((CHUNK, lanes), f32),
                pltpu.VMEM((CHUNK, lanes), f32),
                pltpu.VMEM((8, lanes), f32),
                pltpu.VMEM((CHUNK, lanes), f32),
                pltpu.VMEM((CHUNK, lanes), f32),
                pltpu.VMEM((8, lanes), f32),
                dma((6,)),
                dma((6,)),
                dma((3,)),
                dma((3,)),
            ],
            compiler_params=pltpu.CompilerParams(
                collective_id=sweep, has_side_effects=True, vmem_limit_bytes=24 * 2**20
            ),
            name="residual",
        )(field, current, sigma_rows)

    def solve(field, res, last):
        extra = [sigma_rows] if last else []
        out = pl.pallas_call(
            functools.partial(solve_kernel, dims, last),
            out_shape=(whole, slabs) if last else (whole,),
            in_specs=[smem, vmem, vmem, hbm, vmem, vmem] + [vmem] * len(extra),
            out_specs=(vmem, vmem) if last else (vmem,),
            scratch_shapes=[
                pltpu.VMEM((nseg, blk, blk), jnp.bfloat16),
                pltpu.VMEM(((cz + blk // 24 + 2) * 24, lanes), f32),
                pltpu.VMEM((nseg * blk, lanes), f32),
                pltpu.VMEM((cz * 24, lanes), f32),
            ]
            + ([pltpu.VMEM((cz + cap, lanes), f32)] if last else [])
            + [dma((nseg,))],
            compiler_params=pltpu.CompilerParams(vmem_limit_bytes=40 * 2**20),
            name="solve",
        )(ints, field, res, solvers, diag, group, *extra)
        return out if last else out[0]

    field = planes_first(earlier_edge_voltage)
    current = planes_first(coil_drive_current)
    sigma_rows = planes_first(sigma_omega_cellwise)[0]
    solvers = subdomain_inverse_full[0, 0, 0]
    for sweep in range(SWEEPS - 1):
        field = solve(field, residual(field, sweep), False)
    field, outgoing = solve(field, residual(field, SWEEPS - 1), True)
    layers = jnp.arange(cap)[:, None, None]
    ends = jnp.broadcast_to((layers + 1 == my_len).astype(f32), (cap, owners, lanes))
    tiles = jax.ShapeDtypeStruct((cap, owners, lanes), f32)
    heat, returned = pl.pallas_call(
        functools.partial(heat_kernel, dims),
        out_shape=(tiles, slabs),
        in_specs=[vmem] * 4,
        out_specs=(vmem, vmem),
        scratch_shapes=[
            pltpu.VMEM((owners * cap, lanes), f32),
            pltpu.VMEM((owners * cap, lanes), f32),
            pltpu.VMEM((cap + 2, owners, lanes), f32),
            pltpu.VMEM((cap + 2, owners, lanes), f32),
            pltpu.VMEM((SECTIONS, 2, owners, lanes), f32),
            pltpu.VMEM((SECTIONS, 2, owners, lanes), f32),
            pltpu.VMEM((owners * cap, lanes), f32),
            pltpu.VMEM((owners * cap, lanes), f32),
            pltpu.VMEM((owners * cap, lanes), f32),
            dma((2, owners - 1)),
            dma((2, owners - 1)),
            dma((SECTIONS, 2)),
            dma((SECTIONS, 2)),
        ],
        compiler_params=pltpu.CompilerParams(
            collective_id=SWEEPS, has_side_effects=True, vmem_limit_bytes=24 * 2**20
        ),
        name="heat",
    )(outgoing, onto_tiles(warming_amount), onto_tiles(heat_spreading_coef), ends)
    heat = jnp.where(layers < my_len, heat, 0.0)
    sigma = sigma_rows * returned[back]
    field_new = jnp.swapaxes(field, 1, 2).reshape(6, cx, cy, cz)
    renewed_sigma = sigma.T.reshape(cx, cy, cz)
    heat = jnp.transpose(heat.reshape(cap, gxc, gyc, cx, cy), (0, 1, 3, 2, 4))
    return (field_new, heat.reshape(1, 1, 1, cap, gxc * cx, gyc * cy), renewed_sigma)


def solution(mesh):
    shape = (mesh.shape["gx"], mesh.shape["gy"], mesh.shape["gz"])
    return jax.shard_map(
        functools.partial(body, shape),
        mesh=mesh,
        in_specs=(
            P(None, "gx", "gy", "gz"),
            P(None, "gx", "gy", "gz"),
            P("gx", "gy", "gz"),
            P("gx", "gy", "gz", None, None, None),
            P("gx", "gy", "gz", None, None),
            P("gx", "gy", "gz", None),
            P("gz", None),
            P("gx", "gy", "gz", None, None, None),
            P("gx", "gy", "gz", None, None, None),
        ),
        out_specs=(
            P(None, "gx", "gy", "gz"),
            P("gx", "gy", "gz", None, None, None),
            P("gx", "gy", "gz"),
        ),
        check_vma=False,
    )
```

```python
import functools

import jax
import jax.numpy as jnp
from jax import lax
from jax.experimental import pallas as pl
from jax.experimental.pallas import tpu as pltpu
from jax.sharding import PartitionSpec as P

SWEEPS = 2
SECTIONS = 4
MESH = pl.DeviceIdType.MESH

mass_shift = 1.0
solver_scale = 0.2
coupling_scale = 0.05
time_step = 2.5
heat_drop = 0.15

CHUNK = 64
PAD = 8


def roll(value, shift, axis):
    size = value.shape[axis]
    shift = shift % size
    return value if shift == 0 else pltpu.roll(value, shift, axis)


def remote(src, dst, ssem, rsem, device):
    return pltpu.make_async_remote_copy(
        src_ref=src,
        dst_ref=dst,
        send_sem=ssem,
        recv_sem=rsem,
        device_id=device,
        device_id_type=MESH,
    )


def when_all(entries, act):
    for there, item in entries:

        @pl.when(there)
        def _():
            act(item)


def start_all(entries):
    when_all(entries, lambda copy: copy.start())


def wait_sent(entries):
    when_all(entries, lambda copy: copy.wait_send())


def wait_got(entries):
    when_all(entries, lambda copy: copy.wait_recv())


def greet(entries, others=()):
    barrier = pltpu.get_barrier_semaphore()

    def signal(device):
        pl.semaphore_signal(barrier, inc=1, device_id=device, device_id_type=MESH)

    for device in others:
        signal(device)
    when_all(entries, signal)
    peers = sum([there.astype(jnp.int32) for there, _ in entries], jnp.int32(len(others)))
    pl.semaphore_wait(barrier, peers)


def residual_kernel(
    dims,
    e_ref,
    cur_ref,
    sig_ref,
    res_out,
    field,
    div,
    send_x,
    send_y,
    send_z,
    recv_x,
    recv_y,
    recv_z,
    dsend_x,
    dsend_y,
    dsend_z,
    drecv_x,
    drecv_y,
    drecv_z,
    face_send_sem,
    face_recv_sem,
    div_send_sem,
    div_recv_sem,
):
    gxc, gyc, gzc, cx, cy, cz, nseg, blk, cap = dims
    lanes = cx * cy
    chunks = cz // CHUNK
    gx, gy, gz = lax.axis_index("gx"), lax.axis_index("gy"), lax.axis_index("gz")
    f32 = jnp.float32

    sides = {
        "x+": (gx < gxc - 1, (gx + 1, gy, gz)),
        "x-": (gx > 0, (gx - 1, gy, gz)),
        "y+": (gy < gyc - 1, (gx, gy + 1, gz)),
        "y-": (gy > 0, (gx, gy - 1, gz)),
        "z+": (gz < gzc - 1, (gx, gy, gz + 1)),
        "z-": (gz > 0, (gx, gy, gz - 1)),
    }

    for ref in (recv_x, recv_y, recv_z, drecv_x, drecv_y, drecv_z, send_z, dsend_z):
        ref[...] = jnp.zeros_like(ref)

    for c in range(6):
        field[c, pl.ds(PAD, cz)] = e_ref[c]

    lane = lax.broadcasted_iota(jnp.int32, (CHUNK, lanes), 1)
    lane_x = lane // cy
    lane_y = lane % cy

    def face_copies():
        names = ["x+", "x-", "y+", "y-", "z+", "z-"]
        pairs = [
            (send_x.at[0], recv_x.at[0]),
            (send_x.at[1], recv_x.at[1]),
            (send_y.at[0], recv_y.at[0]),
            (send_y.at[1], recv_y.at[1]),
            (send_z.at[0], recv_z.at[0]),
            (send_z.at[1], recv_z.at[1]),
        ]
        copies = [
            remote(src, dst, face_send_sem.at[i], face_recv_sem.at[i], sides[n][1])
            for i, (n, (src, dst)) in enumerate(zip(names, pairs))
        ]
        sends = [(sides[n][0], copy) for n, copy in zip(names, copies)]
        back = ["x-", "x+", "y-", "y+", "z-", "z+"]
        gets = [(sides[n][0], copy) for n, copy in zip(back, copies)]
        return sends, gets

    def div_copies():
        names = ["x-", "y-", "z-"]
        pairs = [
            (dsend_x, drecv_x),
            (dsend_y, drecv_y),
            (dsend_z, drecv_z),
        ]
        copies = [
            remote(src, dst, div_send_sem.at[i], div_recv_sem.at[i], sides[n][1])
            for i, (n, (src, dst)) in enumerate(zip(names, pairs))
        ]
        sends = [(sides[n][0], copy) for n, copy in zip(names, copies)]
        gets = [(sides[n][0], copy) for n, copy in zip(["x+", "y+", "z+"], copies)]
        return sends, gets

    def pack_faces():
        @pl.loop(0, chunks)
        def _(i):
            rows = pl.ds(pl.multiple_of(i * CHUNK, CHUNK), CHUNK)
            inner = pl.ds(pl.multiple_of(i * CHUNK + PAD, 8), CHUNK)
            x_hi = jnp.zeros((CHUNK, lanes), f32)
            x_lo, y_hi, y_lo = x_hi, x_hi, x_hi
            for c in range(6):
                v = field[c, inner]
                here = lane_x == c
                x_hi = jnp.where(here, roll(v, cy * (c - cx + 1), 1), x_hi)
                x_lo = jnp.where(here, roll(v, cy * c, 1), x_lo)
                here = lane_y == c
                y_hi = jnp.where(here, roll(v, c - cy + 1, 1), y_hi)
                y_lo = jnp.where(here, roll(v, c, 1), y_lo)
            send_x[0, rows] = x_hi
            send_x[1, rows] = x_lo
            send_y[0, rows] = y_hi
            send_y[1, rows] = y_lo

        for c in range(6):
            send_z[0, pl.ds(c, 1)] = field[c, pl.ds(PAD + cz - 1, 1)]
            send_z[1, pl.ds(c, 1)] = field[c, pl.ds(PAD, 1)]

    pack_faces()
    greet(list(sides.values()))
    sends, gets = face_copies()
    start_all(sends)

    def keep(there, v):
        return jnp.where(there, v, 0.0)

    for c in range(6):
        field[c, pl.ds(PAD - 1, 1)] = jnp.zeros((1, lanes), f32)
        field[c, pl.ds(PAD + cz, 1)] = jnp.zeros((1, lanes), f32)
    for i in range(chunks):
        z0 = i * CHUNK
        rows = pl.ds(z0, CHUNK)
        sig = sig_ref[rows]
        for c in range(6):
            e = field[c, pl.ds(PAD + z0, CHUNK)]
            turn = sig * field[(c + 3) % 6, pl.ds(PAD + z0, CHUNK)]
            lap = (
                keep(lane_x > 0, roll(e, cy, 1))
                + keep(lane_x < cx - 1, roll(e, -cy, 1))
                + keep(lane_y > 0, roll(e, 1, 1))
                + keep(lane_y < cy - 1, roll(e, -1, 1))
                + field[c, pl.ds(PAD + z0 - 1, CHUNK)]
                + field[c, pl.ds(PAD + z0 + 1, CHUNK)]
                - 6.0 * e
            )
            rest = cur_ref[c, rows] + lap - mass_shift * e
            res_out[c, rows] = rest + turn if c < 3 else rest - turn

    wait_got(gets)
    for c in range(6):
        field[c, pl.ds(PAD - 1, 1)] = recv_z[0, pl.ds(c, 1)]
        field[c, pl.ds(PAD + cz, 1)] = recv_z[1, pl.ds(c, 1)]

    def x_low(v, got, c):
        return jnp.where(lane_x == 0, roll(got, -cy * c, 1), roll(v, cy, 1))

    def x_high(v, got, c):
        return jnp.where(lane_x == cx - 1, roll(got, cy * (cx - 1 - c), 1), roll(v, -cy, 1))

    def y_low(v, got, c):
        return jnp.where(lane_y == 0, roll(got, -c, 1), roll(v, 1, 1))

    def y_high(v, got, c):
        return jnp.where(lane_y == cy - 1, roll(got, cy - 1 - c, 1), roll(v, -1, 1))

    for i in range(chunks):
        z0 = i * CHUNK
        rows = pl.ds(z0, CHUNK)
        for part in range(2):
            cs = [3 * part + k for k in range(3)]
            ex, ey, ez = [field[c, pl.ds(PAD + z0, CHUNK)] for c in cs]
            d = (
                ex
                - x_low(ex, recv_x[0, rows], cs[0])
                + ey
                - y_low(ey, recv_y[0, rows], cs[1])
                + ez
                - field[cs[2], pl.ds(PAD + z0 - 1, CHUNK)]
            )
            div[part, pl.ds(PAD + z0, CHUNK)] = d
            place = 2 * i + part
            dx = roll(d, cy * place, 1)
            dy = roll(d, place, 1)
            if place == 0:
                dsend_x[...] = dx
                dsend_y[...] = dy
            else:
                dsend_x[...] = jnp.where(lane_x == place, dx, dsend_x[...])
                dsend_y[...] = jnp.where(lane_y == place, dy, dsend_y[...])
    for part in range(2):
        dsend_z[pl.ds(part, 1)] = div[part, pl.ds(PAD, 1)]
    dsends, dgets = div_copies()
    start_all(dsends)
    for i in range(chunks):
        rows = pl.ds(i * CHUNK, CHUNK)
        for c in range(6):
            res_out[c, rows] = (
                res_out[c, rows]
                + keep(lane_x == 0, roll(recv_x[0, rows], -cy * c, 1))
                + keep(lane_x == cx - 1, roll(recv_x[1, rows], cy * (cx - 1 - c), 1))
                + keep(lane_y == 0, roll(recv_y[0, rows], -c, 1))
                + keep(lane_y == cy - 1, roll(recv_y[1, rows], cy - 1 - c, 1))
            )
    for c in range(6):
        for row, side in ((0, 0), (cz - 1, 1)):
            at = pl.ds(row, 1)
            res_out[c, at] = res_out[c, at] + recv_z[side, pl.ds(c, 1)]

    wait_got(dgets)
    rim_z = jnp.where(gz == gzc - 1, 1.0, 0.0)
    for part in range(2):
        top = field[3 * part + 2, pl.ds(PAD + cz - 1, 1)]
        div[part, pl.ds(PAD + cz, 1)] = drecv_z[pl.ds(part, 1)] - rim_z * top

    rim = [
        jnp.where((lane_x == cx - 1) & (gx == gxc - 1), 1.0, 0.0),
        jnp.where((lane_y == cy - 1) & (gy == gyc - 1), 1.0, 0.0),
    ]

    for i in range(chunks):
        z0 = i * CHUNK
        rows = pl.ds(z0, CHUNK)
        for part in range(2):
            d = div[part, pl.ds(PAD + z0, CHUNK)]
            place = 2 * i + part
            ahead = [
                x_high(d, drecv_x[...], place),
                y_high(d, drecv_y[...], place),
                div[part, pl.ds(PAD + z0 + 1, CHUNK)],
            ]
            for k in range(3):
                c = 3 * part + k
                e = field[c, pl.ds(PAD + z0, CHUNK)]
                step = ahead[k] - d
                if k < 2:
                    step = step - rim[k] * e
                res_out[c, rows] = res_out[c, rows] - step
    wait_sent(sends)
    wait_sent(dsends)


def solve_kernel(
    dims,
    last,
    ints,
    e_ref,
    res_ref,
    mat_hbm,
    diag_ref,
    group_ref,
    *refs,
):
    gxc, gyc, gzc, cx, cy, cz, nseg, blk, cap = dims
    if last:
        sig_ref, field_out, heat_send, mats, wide, solved, planes, joule, mat_sem = refs
    else:
        field_out, mats, wide, solved, planes, mat_sem = refs
    owners = gxc * gyc
    lanes = cx * cy
    chunks = cz // CHUNK
    at_slot = 2 * nseg
    at_start = at_slot + cz
    f32 = jnp.float32

    copies = [
        pltpu.make_async_copy(mat_hbm.at[s], mats.at[s], mat_sem.at[s]) for s in range(nseg)
    ]
    for copy in copies:
        copy.start()

    lane = lax.broadcasted_iota(jnp.int32, (CHUNK, lanes), 1)
    pick_lane = (lane // cy % 2) * 2 + lane % cy % 2
    block_row = lax.broadcasted_iota(jnp.int32, (blk, lanes), 0)

    wide[pl.ds(0, 24)] = jnp.zeros((24, lanes), f32)
    tail = wide.shape[0] - (cz + 1) * 24
    wide[pl.ds((cz + 1) * 24, tail)] = jnp.zeros((tail, lanes), f32)
    for i in range(chunks):
        z0 = i * CHUNK
        for c in range(6):
            r = res_ref[c, pl.ds(z0, CHUNK)].astype(jnp.bfloat16)
            spread = jnp.dot(r, group_ref[...], preferred_element_type=f32)
            for pq in range(4):
                wide[pl.ds((z0 + 1) * 24 + c * 4 + pq, CHUNK, stride=24), :] = spread[
                    :, pq * lanes : (pq + 1) * lanes
                ]

    for s in range(nseg):
        base = pl.multiple_of(ints[s], 8)
        v = wide[pl.ds(base, blk), :]
        v = jnp.where(block_row < ints[nseg + s], v, 0.0)
        copies[s].wait()
        product = jnp.dot(mats[s], v.astype(jnp.bfloat16), preferred_element_type=f32)
        diag = solver_scale * diag_ref[:, s : s + 1]
        solved[pl.ds(s * blk, blk)] = coupling_scale * product + diag * v

    @pl.loop(0, cz // 8)
    def _(i):
        for j in range(8):
            z = i * 8 + j
            base = pl.multiple_of(ints[at_slot + z], 8)
            planes[pl.ds(pl.multiple_of(z * 24, 8), 24)] = solved[pl.ds(base, 24), :]

    for i in range(chunks):
        z0 = i * CHUNK
        rows = pl.ds(z0, CHUNK)
        total = jnp.zeros((CHUNK, lanes), f32)
        for c in range(6):
            first = z0 * 24 + c * 4
            v = planes[pl.ds(first, CHUNK, stride=24), :]
            for pq in range(1, 4):
                v = jnp.where(pick_lane == pq, planes[pl.ds(first + pq, CHUNK, stride=24), :], v)
            v = e_ref[c, rows] + v
            field_out[c, rows] = v
            total = total + v * v
        if last:
            joule[rows] = 0.5 * sig_ref[rows] * total

    if last:
        joule[pl.ds(cz, cap)] = jnp.zeros((cap, lanes), f32)
        for p in range(owners):
            heat_send[pl.ds(p * cap, cap)] = joule[pl.ds(ints[at_start + p], cap), :]


def heat_kernel(
    dims,
    heat_send,
    temp_ref,
    rate_ref,
    end_ref,
    heat_out,
    back_out,
    heat_recv,
    heat_src,
    state_a,
    state_b,
    end_send,
    end_recv,
    factors,
    back_send,
    back_recv,
    a2a_send_sem,
    a2a_recv_sem,
    end_send_sem,
    end_recv_sem,
):
    gxc, gyc, gzc, cx, cy, cz, nseg, blk, cap = dims
    owners = gxc * gyc
    lanes = cx * cy
    gx, gy, gz = lax.axis_index("gx"), lax.axis_index("gy"), lax.axis_index("gz")
    me = gx * gyc + gy
    f32 = jnp.float32

    last = owners - 1
    up_owner = jnp.where(me == last, 0, me + 1)
    up_gz = jnp.where(me == last, gz + 1, gz)
    down_owner = jnp.where(me == 0, last, me - 1)
    down_gz = jnp.where(me == 0, gz - 1, gz)
    chain = {
        "up": ((me < last) | (gz < gzc - 1), (up_owner // gyc, up_owner % gyc, up_gz)),
        "down": ((me > 0) | (gz > 0), (down_owner // gyc, down_owner % gyc, down_gz)),
    }
    end_recv[...] = jnp.zeros_like(end_recv)

    others = [lax.rem(me + step, owners) for step in range(1, owners)]
    cross_up = (me == last) & (gz < gzc - 1)
    cross_down = (me == 0) & (gz > 0)
    greet(
        [(cross_up, chain["up"][1]), (cross_down, chain["down"][1])],
        [(other // gyc, other % gyc, gz) for other in others],
    )

    def exchange(which, src, dst):
        copies = []
        for step in range(1, owners):
            other = lax.rem(me + step, owners)
            copies.append(
                remote(
                    src.at[pl.ds(pl.multiple_of(other * cap, 8), cap)],
                    dst.at[pl.ds(pl.multiple_of(me * cap, 8), cap)],
                    a2a_send_sem.at[which, step - 1],
                    a2a_recv_sem.at[which, step - 1],
                    (other // gyc, other % gyc, gz),
                )
            )
        for copy in copies:
            copy.start()
        return copies

    def ends(step):
        up = remote(
            end_send.at[step, 0],
            end_recv.at[step, 0],
            end_send_sem.at[step, 0],
            end_recv_sem.at[step, 0],
            chain["up"][1],
        )
        down = remote(
            end_send.at[step, 1],
            end_recv.at[step, 1],
            end_send_sem.at[step, 1],
            end_recv_sem.at[step, 1],
            chain["down"][1],
        )
        sends = [(chain["up"][0], up), (chain["down"][0], down)]
        gets = [(chain["down"][0], up), (chain["up"][0], down)]
        return sends, gets

    def send_ends(step, state):
        total = jnp.zeros((owners, lanes), f32)
        for o in range(0, cap, 8):
            total = total + jnp.sum(end_ref[pl.ds(o, 8)] * state[pl.ds(o + 1, 8)], axis=0)
        end_send[step, 0] = total
        end_send[step, 1] = state[1]
        sends, _ = ends(step)
        start_all(sends)

    mine = pl.ds(pl.multiple_of(me * cap, 8), cap)
    copies = exchange(0, heat_send, heat_recv)

    state_a[pl.ds(1, cap)] = temp_ref[...]
    for state in (state_a, state_b):
        state[0] = jnp.zeros((owners, lanes), f32)
        state[cap + 1] = jnp.zeros((owners, lanes), f32)
    send_ends(0, state_a)

    group = 8
    shape = (group, owners, lanes)
    own = lax.broadcasted_iota(jnp.int32, shape, 1)
    at = lax.broadcasted_iota(jnp.int32, shape, 2)
    at_x, at_y = at // cy, at % cy
    own_y = own % gyc

    def beside(v):
        t = roll(v, cy, 2)
        u = jnp.where(own >= gyc, roll(t, gyc, 1), 0.0)
        total = jnp.where(at_x == 0, u, t)
        t = roll(v, -cy, 2)
        u = jnp.where(own < owners - gyc, roll(t, -gyc, 1), 0.0)
        total = total + jnp.where(at_x == cx - 1, u, t)
        u = jnp.where(own_y > 0, roll(roll(v, 1 - cy, 2), 1, 1), 0.0)
        total = total + jnp.where(at_y == 0, u, roll(v, 1, 2))
        u = jnp.where(own_y < gyc - 1, roll(roll(v, cy - 1, 2), -1, 1), 0.0)
        return total + jnp.where(at_y == cy - 1, u, roll(v, -1, 2))

    coef = time_step / (SECTIONS * SECTIONS)
    states = [state_a, state_b]
    heat_recv[mine] = heat_send[mine]
    for step in range(SECTIONS):
        now, to = states[step % 2], states[1 - step % 2]
        scale = coef if step == 0 else 2.0 * coef
        if step > 0:
            send_ends(step, now)
        sends, gets = ends(step)

        @pl.loop(0, cap // group)
        def _(i):
            t0 = i * group
            rows = pl.ds(pl.multiple_of(t0 * owners, 8), group * owners)
            v = now[pl.ds(t0 + 1, group)]
            up = (1.0 - end_ref[pl.ds(t0, group)]) * now[pl.ds(t0 + 2, group)]
            rate = rate_ref[pl.ds(t0, group)] * (
                beside(v) + now[pl.ds(t0, group)] + up - 6.0 * v
            )
            if step == 0:
                to[pl.ds(t0 + 1, group)] = v + scale * rate
            else:
                rate = rate + heat_src[rows].reshape(shape)
                to[pl.ds(t0 + 1, group)] = 2.0 * v - to[pl.ds(t0 + 1, group)] + scale * rate

        if step == 0:
            for copy in copies:
                copy.wait()
            for p in range(owners):
                heat_src[pl.ds(p, cap, stride=owners), :] = heat_recv[pl.ds(p * cap, cap)]
        wait_got(gets)
        to[1] = to[1] + scale * rate_ref[0] * end_recv[step, 0]

        @pl.loop(0, cap // group)
        def _(i):
            t0 = i * group
            rows = pl.ds(pl.multiple_of(t0 * owners, 8), group * owners)
            above = jnp.broadcast_to(end_recv[step, 1][None], shape)
            extra = rate_ref[pl.ds(t0, group)] * end_ref[pl.ds(t0, group)] * above
            if step == 0:
                extra = extra + heat_src[rows].reshape(shape)
            following = to[pl.ds(t0 + 1, group)] + scale * extra
            to[pl.ds(t0 + 1, group)] = following
            if step == SECTIONS - 1:
                heat_out[pl.ds(t0, group)] = following
                factors[rows] = jnp.exp(-heat_drop * following).reshape(group * owners, lanes)

        wait_sent(sends)

    for p in range(owners):
        back_send[pl.ds(p * cap, cap)] = factors[pl.ds(p, cap, stride=owners), :]
    back_recv[mine] = back_send[mine]
    for copy in exchange(1, back_send, back_recv):
        copy.wait()
    back_out[...] = back_recv[...]


def body(
    mesh_shape,
    earlier_edge_voltage,
    coil_drive_current,
    sigma_omega_cellwise,
    subdomain_inverse_full,
    subdomain_inverse_main,
    subdomain_layer_counts,
    heat_layer_lookup,
    warming_amount,
    heat_spreading_coef,
):
    gxc, gyc, gzc = mesh_shape
    owners = gxc * gyc
    cx, cy, cz = sigma_omega_cellwise.shape
    lanes = cx * cy
    nseg, blk = subdomain_inverse_main.shape[3:]
    cap = warming_amount.shape[3]
    f32 = jnp.float32

    seg_len = subdomain_layer_counts[0, 0, 0]
    starts = jnp.cumsum(seg_len) - seg_len
    plane_ids = jnp.arange(cz, dtype=jnp.int32)
    owner_seg = jnp.sum((starts[None, :] <= plane_ids[:, None]).astype(jnp.int32), axis=1) - 1
    own_start = jnp.sum(
        jnp.where(owner_seg[:, None] == jnp.arange(nseg)[None, :], starts[None, :], 0), axis=1
    )
    slots = owner_seg * blk + (plane_ids - own_start + 1) * 24
    slab_len = heat_layer_lookup[0]
    slab_starts = jnp.cumsum(slab_len) - slab_len
    owner_slab = jnp.sum((slab_starts[None, :] <= plane_ids[:, None]).astype(jnp.int32), axis=1) - 1
    slab_start = jnp.sum(
        jnp.where(owner_slab[:, None] == jnp.arange(owners)[None, :], slab_starts[None, :], 0),
        axis=1,
    )
    back = owner_slab * cap + plane_ids - slab_start
    me = lax.axis_index("gx") * gyc + lax.axis_index("gy")
    my_len = jnp.sum(jnp.where(jnp.arange(owners) == me, slab_len, 0))
    ints = jnp.concatenate(
        [starts * 24, (seg_len + 2) * 24, slots, slab_starts]
    ).astype(jnp.int32)

    def planes_first(a):
        return jnp.swapaxes(a.reshape(-1, lanes, cz), 1, 2)

    def onto_tiles(a):
        a = a[0, 0, 0].reshape(cap, gxc, cx, gyc, cy)
        return jnp.transpose(a, (0, 1, 3, 2, 4)).reshape(cap, owners, lanes)

    diag = jnp.pad(subdomain_inverse_main[0, 0, 0].T, ((0, 0), (0, lanes - nseg)))
    source = jnp.arange(lanes)[:, None]
    target = jnp.arange(4 * lanes)[None, :]
    pq, to = target // lanes, target % lanes
    same = ((source // cy // 2) == (to // cy // 2)) & ((source % cy // 2) == (to % cy // 2))
    part = (source // cy % 2) * 2 + source % cy % 2
    group = (same & (part == pq)).astype(jnp.bfloat16)

    vmem = pl.BlockSpec(memory_space=pltpu.VMEM)
    smem = pl.BlockSpec(memory_space=pltpu.SMEM)
    hbm = pl.BlockSpec(memory_space=pl.ANY)
    dims = (gxc, gyc, gzc, cx, cy, cz, nseg, blk, cap)
    whole = jax.ShapeDtypeStruct((6, cz, lanes), f32)
    slabs = jax.ShapeDtypeStruct((owners * cap, lanes), f32)
    dma = pltpu.SemaphoreType.DMA

    def residual(field, sweep):
        return pl.pallas_call(
            functools.partial(residual_kernel, dims),
            out_shape=whole,
            in_specs=[vmem] * 3,
            out_specs=vmem,
            scratch_shapes=[
                pltpu.VMEM((6, cz + 2 * PAD, lanes), f32),
                pltpu.VMEM((2, cz + 2 * PAD, lanes), f32),
                pltpu.VMEM((2, cz, lanes), f32),
                pltpu.VMEM((2, cz, lanes), f32),
                pltpu.VMEM((2, 8, lanes), f32),
                pltpu.VMEM((2, cz, lanes), f32),
                pltpu.VMEM((2, cz, lanes), f32),
                pltpu.VMEM((2, 8, lanes), f32),
                pltpu.VMEM((CHUNK, lanes), f32),
                pltpu.VMEM((CHUNK, lanes), f32),
                pltpu.VMEM((8, lanes), f32),
                pltpu.VMEM((CHUNK, lanes), f32),
                pltpu.VMEM((CHUNK, lanes), f32),
                pltpu.VMEM((8, lanes), f32),
                dma((6,)),
                dma((6,)),
                dma((3,)),
                dma((3,)),
            ],
            compiler_params=pltpu.CompilerParams(
                collective_id=sweep, has_side_effects=True, vmem_limit_bytes=24 * 2**20
            ),
            name="residual",
        )(field, current, sigma_rows)

    def solve(field, res, last):
        extra = [sigma_rows] if last else []
        out = pl.pallas_call(
            functools.partial(solve_kernel, dims, last),
            out_shape=(whole, slabs) if last else (whole,),
            in_specs=[smem, vmem, vmem, hbm, vmem, vmem] + [vmem] * len(extra),
            out_specs=(vmem, vmem) if last else (vmem,),
            scratch_shapes=[
                pltpu.VMEM((nseg, blk, blk), jnp.bfloat16),
                pltpu.VMEM(((cz + blk // 24 + 2) * 24, lanes), f32),
                pltpu.VMEM((nseg * blk, lanes), f32),
                pltpu.VMEM((cz * 24, lanes), f32),
            ]
            + ([pltpu.VMEM((cz + cap, lanes), f32)] if last else [])
            + [dma((nseg,))],
            compiler_params=pltpu.CompilerParams(vmem_limit_bytes=60 * 2**20),
            name="solve",
        )(ints, field, res, solvers, diag, group, *extra)
        return out if last else out[0]

    field = planes_first(earlier_edge_voltage)
    current = planes_first(coil_drive_current)
    sigma_rows = planes_first(sigma_omega_cellwise)[0]
    solvers = subdomain_inverse_full[0, 0, 0]
    for sweep in range(SWEEPS - 1):
        field = solve(field, residual(field, sweep), False)
    field, outgoing = solve(field, residual(field, SWEEPS - 1), True)
    layers = jnp.arange(cap)[:, None, None]
    ends = jnp.broadcast_to((layers + 1 == my_len).astype(f32), (cap, owners, lanes))
    tiles = jax.ShapeDtypeStruct((cap, owners, lanes), f32)
    heat, returned = pl.pallas_call(
        functools.partial(heat_kernel, dims),
        out_shape=(tiles, slabs),
        in_specs=[vmem] * 4,
        out_specs=(vmem, vmem),
        scratch_shapes=[
            pltpu.VMEM((owners * cap, lanes), f32),
            pltpu.VMEM((owners * cap, lanes), f32),
            pltpu.VMEM((cap + 2, owners, lanes), f32),
            pltpu.VMEM((cap + 2, owners, lanes), f32),
            pltpu.VMEM((SECTIONS, 2, owners, lanes), f32),
            pltpu.VMEM((SECTIONS, 2, owners, lanes), f32),
            pltpu.VMEM((owners * cap, lanes), f32),
            pltpu.VMEM((owners * cap, lanes), f32),
            pltpu.VMEM((owners * cap, lanes), f32),
            dma((2, owners - 1)),
            dma((2, owners - 1)),
            dma((SECTIONS, 2)),
            dma((SECTIONS, 2)),
        ],
        compiler_params=pltpu.CompilerParams(
            collective_id=SWEEPS, has_side_effects=True, vmem_limit_bytes=24 * 2**20
        ),
        name="heat",
    )(outgoing, onto_tiles(warming_amount), onto_tiles(heat_spreading_coef), ends)
    heat = jnp.where(layers < my_len, heat, 0.0)
    sigma = sigma_rows * returned[back]
    field_new = jnp.swapaxes(field, 1, 2).reshape(6, cx, cy, cz)
    renewed_sigma = sigma.T.reshape(cx, cy, cz)
    heat = jnp.transpose(heat.reshape(cap, gxc, gyc, cx, cy), (0, 1, 3, 2, 4))
    return (field_new, heat.reshape(1, 1, 1, cap, gxc * cx, gyc * cy), renewed_sigma)


def solution(mesh):
    shape = (mesh.shape["gx"], mesh.shape["gy"], mesh.shape["gz"])
    return jax.shard_map(
        functools.partial(body, shape),
        mesh=mesh,
        in_specs=(
            P(None, "gx", "gy", "gz"),
            P(None, "gx", "gy", "gz"),
            P("gx", "gy", "gz"),
            P("gx", "gy", "gz", None, None, None),
            P("gx", "gy", "gz", None, None),
            P("gx", "gy", "gz", None),
            P("gz", None),
            P("gx", "gy", "gz", None, None, None),
            P("gx", "gy", "gz", None, None, None),
        ),
        out_specs=(
            P(None, "gx", "gy", "gz"),
            P("gx", "gy", "gz", None, None, None),
            P("gx", "gy", "gz"),
        ),
        check_vma=False,
    )
```
